32 devices in a mesh: chan: 2 (over y), col: 4 (over x, core), row: 4 (over z).
Axes of the slice: x: 2, y: 2, z: 4, core: 2. Of those that a mesh axis runs over, the one named last changes fastest.
Arguments:
- visibilities: bfloat16 [2, 32768], P(None, ('chan', 'col', 'row')), parts along dimension 1, may hold values from -0.01171875 to 0.01171875
- taps: bfloat16 [2, 8, 32768], P(None, None, ('chan', 'col', 'row')), parts along dimension 2, may hold values from 0.049804688 to 1
- targets: int32 [32768, 1], P(('chan', 'col', 'row')), parts along dimension 0, may hold values from 0 to 15; in each aligned block of 1024 rows (0 to 1023, 1024 to 2047, ...) at most 192 rows name the same one
- offsets: int32 [2, 32768], P(None, ('chan', 'col', 'row')), parts along dimension 1, may hold values from 0 to 504
- corr_x: float32 [1536], P('col'), may hold values from 0.5 to 1.5
- corr_y: float32 [1536], P('row'), may hold values from 0.5 to 1.5
- windows: int32 [2, 2], replicated, may hold values from 0 to 31232
Outputs:
- facets: float32 [4, 2, 1536, 1536], P('chan', None, 'col', 'row'), parts along dimension 0
The draws below stay inside these ranges and needn't reach their ends.
There are 2 independent parts, one for each index of `chan`. The reference program is written for one: setup_inputs(seed, part) draws one part's arguments, and reference() takes and returns one part's arrays. A program takes and returns all parts, laid end to end along the dimension named above; an argument that names none is the same for every part. Nothing has to cross between parts.
Inputs may be any that keep to these rules, and one draw needn't show every extreme that they name: `targets`: within the 1024 rows of one device, no subgrid is named by more than 192 rows, a bound that some block reaches.
All inputs are finite; a program needn't handle non-finite values.
Results may differ from the reference program's by a relative error of at most 0.015.
Values may be sent and summed in bfloat16 or wider, within the bound.
A program may use at most 64 MiB of HBM per device.

```python
import math
import jax
import jax.numpy as jnp
import numpy as np
from jax import lax

IMAGE = 32768
SUBGRID = 512
FACET = 1536
KS = 8
NF = 2
R_DEV = 1024
SUBGRIDS = 16
CAP = 192
SLOTS = 3072
TOTAL = 16384
N_COL = 4
N_ROW = 4


def set_ends(array, rng, least, largest):
    extent = array.shape
    spot = [jax.random.randint(jax.random.fold_in(rng, axis), (), 0, extent[axis]) for axis in range(len(extent))]
    array = array.at[tuple(spot)].set(least)
    longest = extent.index(max(extent))
    spot[longest] = (spot[longest] + 1) % extent[longest]
    return array.at[tuple(spot)].set(largest)


def block_levels(own_key, shape, cuts, smallest, top_value):
    gain = 1.0
    for dim, shards_of in cuts:
        steps = jax.random.uniform(jax.random.fold_in(jax.random.fold_in(own_key, 6), dim), (shards_of,), jnp.float32, smallest / len(cuts), top_value / len(cuts))
        gain = gain * jnp.repeat(jnp.exp(steps), shape[dim] // shards_of).reshape((-1,) + (1,) * (len(shape) - 1 - dim))
    return gain


def assign_block(own_key, own, number, rows, amount, top, bound, slope):
    order = jax.random.permutation(own_key, amount)
    heavy_load, ordinary = shares(amount, rows * top, bound, slope, True), shares(amount, rows * top, bound, slope, False)
    places = jnp.arange(amount)

    def named(sizes, offset_by):
        used = int((sizes > 0).sum())
        fixed = max(1, used // 4)
        passed = fixed + (places - fixed + offset_by * (used - fixed)) % max(1, amount - fixed)
        return jnp.zeros((amount,), jnp.int32).at[order[jnp.where(places < fixed, places, passed)]].set(jnp.asarray(sizes, jnp.int32))

    sizes = jnp.where(number % 4 == 0, named(heavy_load, number // 4), named(ordinary, number - number // 4 - 1))
    mixed = jax.random.permutation(jax.random.fold_in(own, 3), amount)
    giver, receiver = mixed[0:amount // 2 * 2:2], mixed[1:amount // 2 * 2:2]
    room = jnp.minimum(sizes[giver] - 1, bound - sizes[receiver]) // 2
    room = jnp.where((giver == order[0]) | (receiver == order[0]) | (sizes[receiver] == 0), 0, jnp.maximum(room, 0))
    passed = jax.random.randint(jax.random.fold_in(own, 4), (amount // 2,), 0, 1 << 20) % (room + 1)
    sizes = sizes.at[giver].add(-passed).at[receiver].add(passed)
    labels = jnp.searchsorted(jnp.cumsum(sizes), jnp.arange(rows * top), side="right").astype(jnp.int32)
    grid = labels.reshape(top, rows).T
    grid = grid[jax.random.permutation(jax.random.fold_in(own, 1), rows)]
    offset_by = jax.random.randint(jax.random.fold_in(own, 2), (rows, 1), 0, top)
    return jnp.take_along_axis(grid, (jnp.arange(top)[None, :] + offset_by) % top, axis=1)


def shares(count, total, limit, slope, full):
    portions = [(1 << 20) // math.isqrt(grade ** slope) + 1 for grade in range(1, count + 1)]
    largest = limit if full else min(limit, max(-(-total // count), total * portions[0] // sum(portions)))
    least = 1 if total - largest >= count - 1 else 0
    given, surplus = [largest] + [least] * (count - 1), total - largest - least * (count - 1)
    while surplus > 0:
        candidates = [i for i in range(1, count) if given[i] < largest] or [i for i in range(1, count) if given[i] < limit]
        whole, remaining = sum([portions[i] for i in candidates]), surplus
        for i in candidates:
            extra = min(limit - given[i], max(1, remaining * portions[i] // whole), surplus)
            given[i] = given[i] + extra
            surplus = surplus - extra
    return np.array(given)


def centred(own_key, shape, width, limit, cuts=(), kind=jnp.bfloat16):
    result = width * jax.random.normal(own_key, shape, jnp.float32)
    if cuts:
        result = result * block_levels(own_key, shape, cuts, -0.22, 0.18)
    return jnp.clip(result, -limit, limit).astype(kind)


def setup_inputs(seed: int = 0, part: int = 0) -> dict:
    splits = jax.random.split(jax.random.key(seed), 8)
    part_splits = jax.random.split(jax.random.fold_in(splits[7], part), 8)
    visibilities = centred(part_splits[0], (2, TOTAL), (0.25 * (R_DEV * SUBGRIDS) ** -0.5), 0.01171875, ((1, 16),))
    taps = jnp.clip(0.049804688 + 0.9501953 * jax.random.uniform(part_splits[1], (2, KS, TOTAL), jnp.float32) ** block_levels(part_splits[1], (2, KS, TOTAL), ((2, 16),), -0.2, 0.2), 0.049804688, 1.0).astype(jnp.bfloat16)
    targets_keys = jax.random.split(jax.random.fold_in(part_splits[2], 1), TOTAL // R_DEV)
    targets_turns = jax.random.permutation(jax.random.fold_in(part_splits[2], 3), TOTAL // R_DEV)
    targets = jax.vmap(lambda own, number: assign_block(jax.random.fold_in(part_splits[2], 2), own, number, R_DEV, SUBGRIDS, 1, CAP, 2))(targets_keys, targets_turns).reshape((TOTAL, 1))
    offsets = set_ends(jax.random.randint(part_splits[3], (2, TOTAL), 0, SUBGRID - KS + 1), jax.random.fold_in(part_splits[3], 1), 0, SUBGRID - KS).astype(jnp.int32)
    corr_x = jnp.clip(1.0 + 0.1 * jax.random.normal(splits[4], (FACET,), jnp.float32), 0.5, 1.5)
    corr_y = jnp.clip(1.0 + 0.1 * jax.random.normal(splits[5], (FACET,), jnp.float32), 0.5, 1.5)
    windows = set_ends(jax.random.randint(splits[6], (NF, 2), 0, IMAGE - FACET + 1), jax.random.fold_in(splits[6], 1), 0, IMAGE - FACET).astype(jnp.int32)
    return {"visibilities": visibilities, "taps": taps, "targets": targets, "offsets": offsets, "corr_x": corr_x, "corr_y": corr_y, "windows": windows}


def phase_table(first, second):
    product = jnp.mod(first[:, None] * second[None, :], IMAGE)
    angle = product.astype(jnp.float32) * (2.0 * math.pi / IMAGE)
    return jnp.cos(angle).astype(jnp.bfloat16), jnp.sin(angle).astype(jnp.bfloat16)


def placed_kernel(kernel_taps, kernel_offsets):
    relative = jnp.arange(SUBGRID, dtype=jnp.int32)[None, :] - kernel_offsets[:, None]
    placed = jnp.zeros(relative.shape, kernel_taps.dtype)
    for tap_index in range(KS):
        placed = jnp.where(relative == tap_index, kernel_taps[tap_index][:, None], placed)
    return placed


def grid_subgrid(values, kernel_taps, kernel_offsets):
    first_kernel = placed_kernel(kernel_taps[0], kernel_offsets[0])
    second_kernel = placed_kernel(kernel_taps[1], kernel_offsets[1])
    weighted = jnp.concatenate([values[0][:, None] * second_kernel, values[1][:, None] * second_kernel], axis=1)
    gridded = jnp.dot(first_kernel.astype(jnp.float32).T, weighted.astype(jnp.float32), precision=lax.Precision.HIGHEST)
    return gridded.astype(jnp.bfloat16)


def row_block(gridded, row_corner, windows, first_row, row_number):
    real_part = gridded[:, :SUBGRID].T
    imag_part = gridded[:, SUBGRID:].T
    stacked = jnp.concatenate([jnp.concatenate([real_part, imag_part], 1), jnp.concatenate([-imag_part, real_part], 1)], 0)
    cell_ids = jnp.mod(row_corner + jnp.arange(SUBGRID, dtype=jnp.int32), IMAGE)
    pieces = []
    for facet_idx in range(NF):
        pixels = windows[facet_idx, 1] + first_row + jnp.arange(row_number, dtype=jnp.int32)
        cosine, sine_part = phase_table(pixels, cell_ids)
        tables = jnp.concatenate([cosine, sine_part], 1)
        pieces.append(jnp.dot(tables.astype(jnp.float32), stacked.astype(jnp.float32), precision=lax.Precision.HIGHEST))
    return jnp.concatenate(pieces, 1)


def column_block(column, col_corner, windows, first_row, row_number):
    cell_ids = jnp.mod(col_corner + jnp.arange(SUBGRID, dtype=jnp.int32), IMAGE)
    pieces = []
    for facet_idx in range(NF):
        facet_block = column[:, facet_idx * 2 * SUBGRID:(facet_idx + 1) * 2 * SUBGRID]
        real_part = facet_block[:, :SUBGRID].T
        imag_part = facet_block[:, SUBGRID:].T
        stacked = jnp.concatenate([jnp.concatenate([real_part, imag_part], 1), jnp.concatenate([-imag_part, real_part], 1)], 0)
        pixels = windows[facet_idx, 0] + first_row + jnp.arange(row_number, dtype=jnp.int32)
        cosine, sine_part = phase_table(pixels, cell_ids)
        tables = jnp.concatenate([cosine, sine_part], 1)
        pieces.append(jnp.dot(tables.astype(jnp.float32), stacked.astype(jnp.float32), precision=lax.Precision.HIGHEST))
    return jnp.concatenate(pieces, 1)


def block_positions(block_targets):
    onehot = (block_targets[:, None] == jnp.arange(SUBGRIDS, dtype=jnp.int32)[None, :]).astype(jnp.int32)
    running = jnp.cumsum(onehot, axis=0)
    return jnp.sum(running * onehot, axis=1) - 1


def reference(visibilities, taps, targets, offsets, corr_x, corr_y, windows):
    blocks = targets[:, 0].reshape(SUBGRIDS, R_DEV)
    position = jax.vmap(block_positions)(blocks).reshape(-1).astype(jnp.int32)
    source = jnp.arange(TOTAL, dtype=jnp.int32) // R_DEV
    destination = (targets[:, 0] * SLOTS + source * CAP + position).astype(jnp.int32)
    rec_values = jnp.zeros((2, SUBGRIDS * SLOTS), visibilities.dtype).at[:, destination].set(visibilities)
    rec_taps = jnp.zeros((2, KS, SUBGRIDS * SLOTS), taps.dtype).at[:, :, destination].set(taps)
    rec_offsets = jnp.zeros((2, SUBGRIDS * SLOTS), jnp.int32).at[:, destination].set(offsets)
    rec_values = jnp.transpose(rec_values.reshape(2, SUBGRIDS, SLOTS), (1, 0, 2))
    rec_taps = jnp.transpose(rec_taps.reshape(2, KS, SUBGRIDS, SLOTS), (2, 0, 1, 3))
    rec_offsets = jnp.transpose(rec_offsets.reshape(2, SUBGRIDS, SLOTS), (1, 0, 2))

    def grid_item(item):
        return grid_subgrid(item[0], item[1], item[2])

    grids = lax.map(grid_item, (rec_values, rec_taps, rec_offsets))
    grids = grids.reshape(N_COL, N_ROW, SUBGRID, 2 * SUBGRID)

    def column_term(column_idx):
        def add_row(running_sum, row_idx):
            corner = jnp.mod((row_idx - N_ROW // 2) * SUBGRID, IMAGE)
            partial_value = row_block(grids[column_idx, row_idx], corner, windows, 0, FACET)
            rounded = lax.optimization_barrier(partial_value.astype(jnp.bfloat16))
            return running_sum + rounded.astype(jnp.float32), None

        start_sum = jnp.zeros((FACET, NF * 2 * SUBGRID), jnp.float32)
        column = lax.scan(add_row, start_sum, jnp.arange(N_ROW, dtype=jnp.int32))[0].astype(jnp.bfloat16)
        corner = jnp.mod((column_idx - N_COL // 2) * SUBGRID, IMAGE)
        partial_value = column_block(column, corner, windows, 0, FACET)
        return lax.optimization_barrier(partial_value.astype(jnp.bfloat16)).astype(jnp.float32)

    def add_column(running_sum, column_idx):
        return running_sum + column_term(column_idx), None

    start_sum = jnp.zeros((FACET, NF * 2 * FACET), jnp.float32)
    summed = lax.scan(add_column, start_sum, jnp.arange(N_COL, dtype=jnp.int32))[0]
    shaped = summed.reshape(FACET, NF, 2, FACET)
    scaled = shaped * corr_x[:, None, None, None] * corr_y[None, None, None, :]
    return jnp.transpose(scaled, (1, 2, 0, 3))
```

```python
import functools
import math

import jax
import jax.numpy as jnp
from jax import lax
from jax.experimental import pallas as pl
from jax.experimental.pallas import tpu as pltpu
from jax.sharding import PartitionSpec as P

IMAGE = 32768
SUBGRID = 512
FACET = 1536
UNIT = 16
CHUNK = 256
FIELDS = 32
STEP = 32
F32 = jnp.float32
BF16 = jnp.bfloat16
NT = (((1,), (1,)), ((), ()))


def sincos(product):
    angle = jnp.mod(product, IMAGE).astype(F32) * (2.0 * math.pi / IMAGE)
    return jnp.cos(angle), jnp.sin(angle)


def split_table(start, count, other):
    coarse = jnp.mod(start + STEP * jnp.arange(count // STEP, dtype=jnp.int32), IMAGE)
    fine = jnp.arange(STEP, dtype=jnp.int32)
    cos_a, sin_a = sincos(coarse[:, None] * other[None, :])
    cos_b, sin_b = sincos(fine[:, None] * other[None, :])
    cos_a, sin_a = cos_a[:, None], sin_a[:, None]
    cosine = (cos_a * cos_b - sin_a * sin_b).astype(BF16).reshape(count, -1)
    sine = (sin_a * cos_b + cos_a * sin_b).astype(BF16).reshape(count, -1)
    return cosine, sine


def pack_kernel(quarter, vis_ref, taps_ref, targets_ref, offsets_ref, out_ref):
    rows = vis_ref.shape[1]
    targets = targets_ref[...]
    named = lax.broadcasted_iota(jnp.int32, (128, rows), 0) == targets
    onehot = jnp.where(named, 1.0, 0.0)
    onehot16 = onehot.astype(BF16)
    counts = lax.dot_general(jnp.ones((16, rows), BF16), onehot16, NT, preferred_element_type=F32)
    units = jnp.floor((counts + (UNIT - 1.0)) * (1.0 / UNIT))
    before = lax.broadcasted_iota(jnp.int32, (128, 128), 0) < lax.broadcasted_iota(
        jnp.int32, (128, 128), 1
    )
    starts = jnp.dot(
        units.astype(BF16), jnp.where(before, 1.0, 0.0).astype(BF16), preferred_element_type=F32
    )
    upto = lax.broadcasted_iota(jnp.int32, (rows, rows), 0) <= lax.broadcasted_iota(
        jnp.int32, (rows, rows), 1
    )
    running = jnp.dot(
        onehot16, jnp.where(upto, 1.0, 0.0).astype(BF16), preferred_element_type=F32
    )
    rank = jnp.sum(running * onehot, axis=0, keepdims=True) - 1.0
    first = jnp.dot(starts.astype(BF16), onehot16, preferred_element_type=F32)[0:1]
    slot = (first * UNIT + rank).astype(jnp.int32)

    lane_pos = lax.broadcasted_iota(jnp.int32, (8, rows), 0)
    placed = []
    for dim in range(2):
        wanted = (lane_pos - offsets_ref[dim : dim + 1, :]) & 7
        value = jnp.zeros((8, rows), F32)
        for tap in range(8):
            row = taps_ref[dim * 8 + tap : dim * 8 + tap + 1, :].astype(F32)
            value = jnp.where(wanted == tap, row, value)
        placed.append(value)
    vis = vis_ref[...].astype(F32)
    offsets = offsets_ref[...]
    upper = (offsets >> 3).astype(F32)
    lower = (offsets & 7).astype(F32)
    extra = jnp.zeros((8, rows), F32)
    for idx, row in enumerate((upper[0:1], lower[0:1], upper[1:2], lower[1:2])):
        extra = jnp.where(lane_pos == idx, row, extra)
    fields = jnp.concatenate(
        [placed[0], placed[1] * vis[0:1], placed[1] * vis[1:2], extra], 0
    ).astype(BF16)
    blank = jnp.zeros_like(fields)
    total = jnp.zeros((quarter, 128), F32)
    slot_ids = lax.broadcasted_iota(jnp.int32, (quarter, rows), 0)
    for part in range(4):
        chosen = jnp.where(slot_ids == slot - part * quarter, 1.0, 0.0).astype(BF16)
        spread = jnp.concatenate([fields if b == part else blank for b in range(4)], 0)
        total += lax.dot_general(chosen, spread, NT, preferred_element_type=F32)
    out_ref[0:quarter, :] = total.astype(BF16)
    which = lax.broadcasted_iota(jnp.int32, (16, 128), 0)
    out_ref[quarter:, :] = jnp.where(
        which == 0, starts, jnp.where(which == 1, units, 0.0)
    ).astype(BF16)


def grid_kernel(
    sources, row_devices, quarter, block, facets,
    starts_ref, units_ref, rows_ref, table_ref, out_ref, packed, grid_sum, sums,
):
    col, row = pl.program_id(0), pl.program_id(1)
    subgrid = col * row_devices + row
    subs = pl.num_programs(0) * row_devices
    per_quarter = quarter // UNIT
    lane_block = lax.broadcasted_iota(jnp.int32, (UNIT, 128), 1) // FIELDS

    def gather(source, pos):
        start = starts_ref[source * subs + subgrid]
        count = units_ref[source * subs + subgrid]

        def four(step, carry):
            for inner in range(4):
                unit = start + step * 4 + inner
                part = unit // per_quarter
                place = pl.multiple_of((unit - part * per_quarter) * UNIT, UNIT)
                data = rows_ref[source, pl.ds(place, UNIT), :]
                data = jnp.where(lane_block == part, data.astype(F32), 0.0).astype(BF16)
                to = pl.multiple_of((pos + step * 4 + inner) * UNIT, UNIT)
                packed[pl.ds(to, UNIT), :] = data
            return carry

        lax.fori_loop(0, (count + 3) // 4, four, 0)
        return pos + count

    total = lax.fori_loop(0, sources, gather, 0)
    packed[pl.ds(pl.multiple_of(total * UNIT, UNIT), CHUNK), :] = jnp.zeros((CHUNK, 128), BF16)
    grid_sum[...] = jnp.zeros_like(grid_sum)

    out_row = lax.broadcasted_iota(jnp.int32, (64, 128), 0)
    lane = lax.broadcasted_iota(jnp.int32, (64, 128), 1) % FIELDS
    source_field = jnp.where(out_row < 24, out_row, 24 + (out_row - 24) // 8)
    pick = jnp.where((source_field == lane) & (out_row < 56), 1.0, 0.0).astype(BF16)
    cell = lax.broadcasted_iota(jnp.int32, (8, CHUNK), 0).astype(F32)

    def chunk(step, carry):
        data = packed[pl.ds(pl.multiple_of(step * CHUNK, CHUNK), CHUNK), :]
        field = lax.dot_general(pick, data, NT, preferred_element_type=F32)
        group_u = field[24:32] + jnp.where(cell < field[32:40], 1.0, 0.0)
        group_v = field[40:48] + jnp.where(cell < field[48:56], 1.0, 0.0)
        val_u, val_r, val_i = field[0:8], field[8:16], field[16:24]
        kern_u, kern_r, kern_i = [], [], []
        for g in range(SUBGRID // 8):
            hit_v = group_v == float(g)
            kern_u.append(jnp.where(group_u == float(g), val_u, 0.0))
            kern_r.append(jnp.where(hit_v, val_r, 0.0))
            kern_i.append(jnp.where(hit_v, val_i, 0.0))
        left = jnp.concatenate(kern_u, 0).astype(BF16)
        right = jnp.concatenate(kern_r + kern_i, 0).astype(BF16)
        grid_sum[...] += lax.dot_general(left, right, NT, preferred_element_type=F32)
        return carry

    lax.fori_loop(0, (total * UNIT + CHUNK - 1) // CHUNK, chunk, 0)

    @pl.when(row == 0)
    def _():
        sums[...] = jnp.zeros_like(sums)

    table = table_ref[...]
    real = jnp.dot(grid_sum[:, :SUBGRID].astype(BF16), table, preferred_element_type=F32)
    imag = jnp.dot(grid_sum[:, SUBGRID:].astype(BF16), table, preferred_element_type=F32)
    for f in range(facets):
        lo, mid, hi = 2 * f * block, (2 * f + 1) * block, (2 * f + 2) * block
        sums[:, lo:mid] += real[:, lo:mid] - imag[:, mid:hi]
        sums[:, mid:hi] += real[:, mid:hi] + imag[:, lo:mid]

    @pl.when(row == row_devices - 1)
    def _():
        for f in range(facets):
            out_ref[f] = sums[:, 2 * f * block : 2 * (f + 1) * block].astype(BF16)


def column_kernel(block, cos_ref, sin_ref, part_ref, out_ref):
    value = part_ref[0]
    first = jnp.dot(cos_ref[0, 0], value, preferred_element_type=F32)
    second = jnp.dot(sin_ref[0, 0], value, preferred_element_type=F32)
    out_ref[0, 0, 0] = (first[:, :block] - second[:, block:]).astype(BF16)
    out_ref[0, 0, 1] = (first[:, block:] + second[:, :block]).astype(BF16)


def body(visibilities, taps, targets, offsets, corr_x, corr_y, windows):
    cols = lax.axis_size("col")
    row_devices = lax.axis_size("row")
    subgrids = cols * row_devices
    sources = subgrids
    rows = targets.shape[0]
    cap = 3 * rows // subgrids
    half = cols // 2
    own_col = lax.axis_index("col")
    own_row = lax.axis_index("row")
    core = lax.rem(own_col, 2)
    facets = windows.shape[0]
    block = FACET // row_devices
    pix_rows = FACET // cols
    quarter = -(-(rows + subgrids * (UNIT - 1)) // (4 * UNIT)) * UNIT

    packed = pl.pallas_call(
        functools.partial(pack_kernel, quarter),
        out_shape=jax.ShapeDtypeStruct((quarter + 16, 128), BF16),
        compiler_params=pltpu.CompilerParams(vmem_limit_bytes=40 << 20),
        name="pack_rows",
    )(visibilities, taps.reshape(-1, rows), targets.reshape(1, rows), offsets)
    gathered = lax.all_gather(packed, ("col", "row"), axis=0, tiled=False)

    cells = jnp.int32(IMAGE - row_devices // 2 * SUBGRID)
    pieces = []
    for f in range(facets):
        pixels = windows[f, 1] + own_row * block + jnp.arange(block, dtype=jnp.int32)
        pieces += list(split_table(cells, row_devices * SUBGRID, pixels))
    row_table = jnp.concatenate(pieces, 1)
    first_cell = (core * half - cols // 2) * SUBGRID
    col_cells = jnp.mod(first_cell + jnp.arange(half * SUBGRID, dtype=jnp.int32), IMAGE)
    cosines, sines = [], []
    for f in range(facets):
        for who in (own_col + 1 - 2 * core, own_col):
            cosine, sine = split_table(windows[f, 0] + who * pix_rows, pix_rows, col_cells)
            cosines.append(cosine)
            sines.append(sine)
    col_cos = jnp.stack(cosines).reshape(facets, 2, pix_rows, half * SUBGRID)
    col_sin = jnp.stack(sines).reshape(facets, 2, pix_rows, half * SUBGRID)

    own_subs = half * row_devices
    meta = gathered[:, quarter : quarter + 2, :].astype(jnp.int32)
    meta = lax.dynamic_slice(meta, (0, 0, core * own_subs), (sources, 2, own_subs))
    starts = meta[:, 0].reshape(-1)
    units = meta[:, 1].reshape(-1)
    room = sources * (-(-cap // UNIT)) * UNIT + CHUNK + 4 * UNIT
    width = facets * 2 * block
    parts = pl.pallas_call(
        functools.partial(grid_kernel, sources, row_devices, quarter, block, facets),
        grid_spec=pltpu.PrefetchScalarGridSpec(
            num_scalar_prefetch=2,
            grid=(half, row_devices),
            in_specs=[
                pl.BlockSpec(
                    (sources, quarter + 16, 128),
                    lambda c, r, *_: (0, 0, 0),
                    pipeline_mode=pl.Buffered(1),
                ),
                pl.BlockSpec((SUBGRID, width), lambda c, r, *_: (r, 0)),
            ],
            out_specs=pl.BlockSpec((facets, SUBGRID, 2 * block), lambda c, r, *_: (0, c, 0)),
            scratch_shapes=[
                pltpu.VMEM((room, 128), BF16),
                pltpu.VMEM((SUBGRID, 2 * SUBGRID), F32),
                pltpu.VMEM((SUBGRID, width), F32),
            ],
        ),
        out_shape=jax.ShapeDtypeStruct((facets, half * SUBGRID, 2 * block), BF16),
        compiler_params=pltpu.CompilerParams(vmem_limit_bytes=56 << 20),
        name="grid_rows",
    )(starts, units, gathered, row_table)

    depth = half * SUBGRID
    table_spec = pl.BlockSpec((1, 1, pix_rows, depth), lambda w, f: (f, w, 0, 0))
    images = pl.pallas_call(
        functools.partial(column_kernel, block),
        grid=(2, facets),
        in_specs=[
            table_spec,
            table_spec,
            pl.BlockSpec((1, depth, 2 * block), lambda w, f: (f, 0, 0)),
        ],
        out_specs=pl.BlockSpec((1, 1, 2, pix_rows, block), lambda w, f: (w, f, 0, 0, 0)),
        out_shape=jax.ShapeDtypeStruct((2, facets, 2, pix_rows, block), BF16),
        compiler_params=pltpu.CompilerParams(vmem_limit_bytes=56 << 20),
        name="column_sums",
    )(col_cos, col_sin, parts)
    swap = [(c, c ^ 1) for c in range(cols)]
    other = lax.ppermute(images[0], "col", swap)
    summed = images[1].astype(F32) + other.astype(F32)
    return summed * corr_x[None, None, :, None] * corr_y[None, None, None, :]


def solution(mesh):
    in_specs = (
        P(None, ("chan", "col", "row")),
        P(None, None, ("chan", "col", "row")),
        P(("chan", "col", "row"), None),
        P(None, ("chan", "col", "row")),
        P("col"),
        P("row"),
        P(),
    )
    out_specs = P("chan", None, "col", "row")
    return jax.shard_map(body, mesh=mesh, in_specs=in_specs, out_specs=out_specs, check_vma=False)
```

```python
import functools
import math

import jax
import jax.numpy as jnp
from jax import lax
from jax.experimental import pallas as pl
from jax.experimental.pallas import tpu as pltpu
from jax.sharding import PartitionSpec as P

IMAGE = 32768
SUBGRID = 512
FACET = 1536
UNIT = 16
CHUNK = 512
FIELDS = 32
STEP = 32
F32 = jnp.float32
BF16 = jnp.bfloat16
NT = (((1,), (1,)), ((), ()))


def sincos(product):
    quarter = IMAGE // 4
    turn = (product & (IMAGE - 1)) + quarter // 2
    turns = turn // quarter
    x = (turn - turns * quarter - quarter // 2).astype(F32) * (2.0 * math.pi / IMAGE)
    y = x * x
    cosine = 1.0 + y * (-1 / 2 + y * (1 / 24 + y * (-1 / 720 + y * (1 / 40320))))
    sine = x * (1.0 + y * (-1 / 6 + y * (1 / 120 + y * (-1 / 5040 + y * (1 / 362880)))))
    odd = (turns & 1) == 1
    first, second = jnp.where(odd, sine, cosine), jnp.where(odd, cosine, sine)
    flip_cos = ((turns + 1) & 2) == 2
    flip_sin = (turns & 2) == 2
    return jnp.where(flip_cos, -first, first), jnp.where(flip_sin, -second, second)


def coarse_ids(start, count, axis_len):
    steps = lax.broadcasted_iota(jnp.int32, (count // STEP, axis_len), 0)
    return (start + STEP * steps) & (IMAGE - 1)


def fill_table(coarse_cos, coarse_sin, fine, write):
    fine_cos, fine_sin = fine

    def one(step, carry):
        cos_a, sin_a = coarse_cos[pl.ds(step, 1), :], coarse_sin[pl.ds(step, 1), :]
        write(
            pl.ds(pl.multiple_of(step * STEP, STEP), STEP),
            (cos_a * fine_cos - sin_a * fine_sin).astype(BF16),
            (sin_a * fine_cos + cos_a * fine_sin).astype(BF16),
        )
        return carry

    lax.fori_loop(0, coarse_cos.shape[0], one, 0)


def spread_kernel(
    quarter, cols, row_devices, block, facets, win_ref, vis_ref, taps_ref, targets_ref,
    offsets_ref, all_ref, row_table, col_cos, col_sin, *scratch,
):
    row_cos, row_sin, pix_cos, pix_sin = scratch[:4]
    send_row, recv_row, send_chip, recv_chip, send_core, recv_core = scratch[4:]
    own_col, own_row = lax.axis_index("col"), lax.axis_index("row")
    chips = cols // 2
    chip, core = own_col // 2, own_col % 2
    barrier = pltpu.get_barrier_semaphore()
    row_peers = [lax.rem(own_row + k, row_devices) for k in range(1, row_devices)]
    chip_peers = [lax.rem(chip + p, chips) for p in range(1, chips)]
    for peer in row_peers:
        pl.semaphore_signal(
            barrier, inc=1, device_id={"row": peer}, device_id_type=pl.DeviceIdType.MESH
        )
    for peer in chip_peers:
        pl.semaphore_signal(
            barrier, inc=1, device_id={"col": peer * 2 + core}, device_id_type=pl.DeviceIdType.MESH
        )
    pl.semaphore_signal(
        barrier, inc=1, device_id={"col": chip * 2 + 1 - core}, device_id_type=pl.DeviceIdType.MESH
    )

    pack_rows(quarter, vis_ref, taps_ref, targets_ref, offsets_ref, all_ref.at[chip, core, own_row])
    pl.semaphore_wait(barrier, row_devices - 1 + chips - 1 + 1)

    def send(ref, send_sem, recv_sem, device):
        copy = pltpu.make_async_remote_copy(
            src_ref=ref, dst_ref=ref, send_sem=send_sem, recv_sem=recv_sem,
            device_id=device, device_id_type=pl.DeviceIdType.MESH,
        )
        copy.start()
        return copy

    def row_of(k):
        return lax.rem(own_row + row_devices - k, row_devices)

    def to_chips(k):
        ref = all_ref.at[chip, core, row_of(k)]
        return [
            send(
                ref, send_chip.at[k, p - 1], recv_chip.at[k, p - 1],
                {"col": chip_peers[p - 1] * 2 + core},
            )
            for p in range(1, chips)
        ]

    def to_core(k, p):
        ref = all_ref.at[lax.rem(chip + chips - p, chips), core, row_of(k)]
        return send(ref, send_core.at[k, p], recv_core.at[k, p], {"col": chip * 2 + 1 - core})

    by_row = [
        send(
            all_ref.at[chip, core, own_row], send_row.at[k - 1], recv_row.at[k - 1],
            {"row": row_peers[k - 1]},
        )
        for k in range(1, row_devices)
    ]
    by_chip = {0: to_chips(0)}
    by_core = [to_core(0, 0)]

    pix_rows = col_cos.shape[2]
    depth = col_cos.shape[3]
    first_cell = (core * (depth // SUBGRID) - chips) * SUBGRID
    cells = (first_cell + lax.broadcasted_iota(jnp.int32, (1, depth), 1)) & (IMAGE - 1)
    fine_cells = sincos(lax.broadcasted_iota(jnp.int32, (STEP, depth), 0) * cells)
    corner = IMAGE - row_devices // 2 * SUBGRID
    for stage in range(facets + 1):
        if stage == 1:
            for k in range(1, row_devices):
                by_row[k - 1].wait_recv()
                by_chip[k] = to_chips(k)
                by_core.append(to_core(k, 0))
        if stage == 2:
            for k in range(row_devices):
                for p in range(1, chips):
                    by_chip[k][p - 1].wait_recv()
                    by_core.append(to_core(k, p))
        if stage == facets:
            break
        f = stage
        pixels = win_ref[f, 1] + own_row * block + lax.broadcasted_iota(jnp.int32, (1, block), 1)
        fine = sincos(lax.broadcasted_iota(jnp.int32, (STEP, block), 0) * pixels)
        row_cos[...], row_sin[...] = sincos(
            coarse_ids(corner, row_devices * SUBGRID, block) * pixels
        )

        def write_row(place, cosine, sine):
            row_table[place, 2 * f * block : (2 * f + 1) * block] = cosine
            row_table[place, (2 * f + 1) * block : (2 * f + 2) * block] = sine

        fill_table(row_cos, row_sin, fine, write_row)
        for who, holder in enumerate((chip * 2 + 1 - core, own_col)):
            first = win_ref[f, 0] + holder * pix_rows
            pix_cos[...], pix_sin[...] = sincos(coarse_ids(first, pix_rows, depth) * cells)

            def write_col(place, cosine, sine):
                col_cos[f, who, place, :] = cosine
                col_sin[f, who, place, :] = sine

            fill_table(pix_cos, pix_sin, fine_cells, write_col)
    for copy in by_core:
        copy.wait_recv()
    for copy in by_row + [c for k in by_chip for c in by_chip[k]] + by_core:
        copy.wait_send()


def pack_rows(quarter, vis_ref, taps_ref, targets_ref, offsets_ref, out_ref):
    rows = vis_ref.shape[1]
    targets = targets_ref[...]
    named = lax.broadcasted_iota(jnp.int32, (128, rows), 0) == targets
    onehot = jnp.where(named, 1.0, 0.0)
    onehot16 = onehot.astype(BF16)
    counts = lax.dot_general(jnp.ones((16, rows), BF16), onehot16, NT, preferred_element_type=F32)
    units = jnp.floor((counts + (UNIT - 1.0)) * (1.0 / UNIT))
    before = lax.broadcasted_iota(jnp.int32, (128, 128), 0) < lax.broadcasted_iota(
        jnp.int32, (128, 128), 1
    )
    starts = jnp.dot(
        units.astype(BF16), jnp.where(before, 1.0, 0.0).astype(BF16), preferred_element_type=F32
    )
    upto = lax.broadcasted_iota(jnp.int32, (rows, rows), 0) <= lax.broadcasted_iota(
        jnp.int32, (rows, rows), 1
    )
    running = jnp.dot(
        onehot16, jnp.where(upto, 1.0, 0.0).astype(BF16), preferred_element_type=F32
    )
    rank = jnp.sum(running * onehot, axis=0, keepdims=True) - 1.0
    first = jnp.dot(starts.astype(BF16), onehot16, preferred_element_type=F32)[0:1]
    slot = (first * UNIT + rank).astype(jnp.int32)

    lane_pos = lax.broadcasted_iota(jnp.int32, (8, rows), 0)
    placed = []
    for dim in range(2):
        wanted = (lane_pos - offsets_ref[dim : dim + 1, :]) & 7
        value = jnp.zeros((8, rows), F32)
        for tap in range(8):
            row = taps_ref[dim * 8 + tap : dim * 8 + tap + 1, :].astype(F32)
            value = jnp.where(wanted == tap, row, value)
        placed.append(value)
    vis = vis_ref[...].astype(F32)
    offsets = offsets_ref[...]
    upper = (offsets >> 3).astype(F32)
    lower = (offsets & 7).astype(F32)
    extra = jnp.zeros((8, rows), F32)
    for idx, row in enumerate((upper[0:1], lower[0:1], upper[1:2], lower[1:2])):
        extra = jnp.where(lane_pos == idx, row, extra)
    fields = jnp.concatenate(
        [placed[0], placed[1] * vis[0:1], placed[1] * vis[1:2], extra], 0
    ).astype(BF16)
    blank = jnp.zeros_like(fields)
    total = jnp.zeros((quarter, 128), F32)
    slot_ids = lax.broadcasted_iota(jnp.int32, (quarter, rows), 0)
    for part in range(4):
        chosen = jnp.where(slot_ids == slot - part * quarter, 1.0, 0.0).astype(BF16)
        spread = jnp.concatenate([fields if b == part else blank for b in range(4)], 0)
        total += lax.dot_general(chosen, spread, NT, preferred_element_type=F32)
    out_ref[0:quarter, :] = total.astype(BF16)
    which = lax.broadcasted_iota(jnp.int32, (16, 128), 0)
    out_ref[quarter:, :] = jnp.where(
        which == 0, starts, jnp.where(which == 1, units, 0.0)
    ).astype(BF16)


def grid_kernel(
    sources, row_devices, quarter, block, facets,
    starts_ref, units_ref, rows_ref, table_ref, out_ref, packed, grid_sum, grids,
):
    col, row = pl.program_id(0), pl.program_id(1)
    subgrid = col * row_devices + row
    subs = pl.num_programs(0) * row_devices
    per_quarter = quarter // UNIT
    lane_block = lax.broadcasted_iota(jnp.int32, (UNIT, 128), 1) // FIELDS

    def gather(source, pos):
        start = starts_ref[source * subs + subgrid]
        count = units_ref[source * subs + subgrid]

        def four(step, carry):
            for inner in range(4):
                unit = start + step * 4 + inner
                part = unit // per_quarter
                place = pl.multiple_of((unit - part * per_quarter) * UNIT, UNIT)
                data = rows_ref[source, pl.ds(place, UNIT), :]
                data = jnp.where(lane_block == part, data.astype(F32), 0.0).astype(BF16)
                to = pl.multiple_of((pos + step * 4 + inner) * UNIT, UNIT)
                packed[pl.ds(to, UNIT), :] = data
            return carry

        lax.fori_loop(0, (count + 3) // 4, four, 0)
        return pos + count

    total = lax.fori_loop(0, sources, gather, 0)
    packed[pl.ds(pl.multiple_of(total * UNIT, UNIT), CHUNK), :] = jnp.zeros((CHUNK, 128), BF16)
    grid_sum[...] = jnp.zeros_like(grid_sum)

    out_row = lax.broadcasted_iota(jnp.int32, (64, 128), 0)
    lane = lax.broadcasted_iota(jnp.int32, (64, 128), 1) % FIELDS
    source_field = jnp.where(out_row < 24, out_row, 24 + (out_row - 24) // 8)
    pick = jnp.where((source_field == lane) & (out_row < 56), 1.0, 0.0).astype(BF16)
    cell = lax.broadcasted_iota(jnp.int32, (8, CHUNK), 0).astype(F32)

    def chunk(step, carry):
        data = packed[pl.ds(pl.multiple_of(step * CHUNK, CHUNK), CHUNK), :]
        field = lax.dot_general(pick, data, NT, preferred_element_type=F32)
        group_u = field[24:32] + jnp.where(cell < field[32:40], 1.0, 0.0)
        group_v = field[40:48] + jnp.where(cell < field[48:56], 1.0, 0.0)
        val_u, val_r, val_i = field[0:8], field[8:16], field[16:24]
        kern_u, kern_r, kern_i = [], [], []
        for g in range(SUBGRID // 8):
            hit_v = group_v == float(g)
            kern_u.append(jnp.where(group_u == float(g), val_u, 0.0))
            kern_r.append(jnp.where(hit_v, val_r, 0.0))
            kern_i.append(jnp.where(hit_v, val_i, 0.0))
        left = jnp.concatenate(kern_u, 0).astype(BF16)
        right = jnp.concatenate(kern_r + kern_i, 0).astype(BF16)
        grid_sum[...] += lax.dot_general(left, right, NT, preferred_element_type=F32)
        return carry

    lax.fori_loop(0, (total * UNIT + CHUNK - 1) // CHUNK, chunk, 0)

    place = pl.ds(pl.multiple_of(row * SUBGRID, SUBGRID), SUBGRID)
    grids[0:SUBGRID, place] = grid_sum[:, :SUBGRID].astype(BF16)
    grids[SUBGRID:, place] = grid_sum[:, SUBGRID:].astype(BF16)

    @pl.when(row == row_devices - 1)
    def _():
        for f in range(facets):
            table = table_ref[:, 2 * f * block : 2 * (f + 1) * block]
            product = jnp.dot(grids[...], table, preferred_element_type=F32)
            real, imag = product[:SUBGRID], product[SUBGRID:]
            out_ref[f, :, :block] = (real[:, :block] - imag[:, block:]).astype(BF16)
            out_ref[f, :, block:] = (real[:, block:] + imag[:, :block]).astype(BF16)


def column_kernel(block, cos_ref, sin_ref, part_ref, out_ref):
    value = part_ref[0]
    first = jnp.dot(cos_ref[0, 0], value, preferred_element_type=F32)
    second = jnp.dot(sin_ref[0, 0], value, preferred_element_type=F32)
    out_ref[0, 0] = (first[:, :block] - second[:, block:]).astype(out_ref.dtype)
    out_ref[0, 1] = (first[:, block:] + second[:, :block]).astype(out_ref.dtype)


def body(visibilities, taps, targets, offsets, corr_x, corr_y, windows):
    cols = lax.axis_size("col")
    row_devices = lax.axis_size("row")
    subgrids = cols * row_devices
    sources = subgrids
    rows = targets.shape[0]
    cap = 3 * rows // subgrids
    half = cols // 2
    own_col = lax.axis_index("col")
    core = lax.rem(own_col, 2)
    facets = windows.shape[0]
    block = FACET // row_devices
    pix_rows = FACET // cols
    quarter = -(-(rows + subgrids * (UNIT - 1)) // (4 * UNIT)) * UNIT

    chips = cols // 2
    depth = half * SUBGRID
    width = facets * 2 * block
    vmem = pl.BlockSpec(memory_space=pltpu.VMEM)
    all_rows, row_table, col_cos, col_sin = pl.pallas_call(
        functools.partial(spread_kernel, quarter, cols, row_devices, block, facets),
        in_specs=[pl.BlockSpec(memory_space=pltpu.SMEM)] + [vmem] * 4,
        out_specs=[vmem] * 4,
        out_shape=[
            jax.ShapeDtypeStruct((chips, 2, row_devices, quarter + 16, 128), BF16),
            jax.ShapeDtypeStruct((row_devices * SUBGRID, width), BF16),
            jax.ShapeDtypeStruct((facets, 2, pix_rows, depth), BF16),
            jax.ShapeDtypeStruct((facets, 2, pix_rows, depth), BF16),
        ],
        scratch_shapes=[pltpu.VMEM((row_devices * SUBGRID // STEP, block), F32)] * 2
        + [pltpu.VMEM((pix_rows // STEP, depth), F32)] * 2
        + [pltpu.SemaphoreType.DMA((max(row_devices - 1, 1),))] * 2
        + [pltpu.SemaphoreType.DMA((row_devices, max(chips - 1, 1)))] * 2
        + [pltpu.SemaphoreType.DMA((row_devices, chips))] * 2,
        compiler_params=pltpu.CompilerParams(
            vmem_limit_bytes=60 << 20, collective_id=0, has_side_effects=True
        ),
        name="spread_rows",
    )(windows, visibilities, taps.reshape(-1, rows), targets.reshape(1, rows), offsets)
    gathered = all_rows.reshape(sources, quarter + 16, 128)

    own_subs = half * row_devices
    meta = gathered[:, quarter : quarter + 2, :].astype(jnp.int32)
    meta = lax.dynamic_slice(meta, (0, 0, core * own_subs), (sources, 2, own_subs))
    starts = meta[:, 0].reshape(-1)
    units = meta[:, 1].reshape(-1)
    room = sources * (-(-cap // UNIT)) * UNIT + CHUNK + 4 * UNIT
    parts = pl.pallas_call(
        functools.partial(grid_kernel, sources, row_devices, quarter, block, facets),
        grid_spec=pltpu.PrefetchScalarGridSpec(
            num_scalar_prefetch=2,
            grid=(half, row_devices),
            in_specs=[
                pl.BlockSpec(
                    (sources, quarter + 16, 128),
                    lambda c, r, *_: (0, 0, 0),
                    pipeline_mode=pl.Buffered(1),
                ),
                pl.BlockSpec(
                    (row_devices * SUBGRID, width),
                    lambda c, r, *_: (0, 0),
                    pipeline_mode=pl.Buffered(1),
                ),
            ],
            out_specs=pl.BlockSpec((facets, SUBGRID, 2 * block), lambda c, r, *_: (0, c, 0)),
            scratch_shapes=[
                pltpu.VMEM((room, 128), BF16),
                pltpu.VMEM((SUBGRID, 2 * SUBGRID), F32),
                pltpu.VMEM((2 * SUBGRID, row_devices * SUBGRID), BF16),
            ],
        ),
        out_shape=jax.ShapeDtypeStruct((facets, half * SUBGRID, 2 * block), BF16),
        compiler_params=pltpu.CompilerParams(vmem_limit_bytes=56 << 20),
        name="grid_rows",
    )(starts, units, gathered, row_table)

    def column_sums(who, dtype):
        table_spec = pl.BlockSpec((1, 1, pix_rows, depth), lambda f: (f, who, 0, 0))
        return pl.pallas_call(
            functools.partial(column_kernel, block),
            grid=(facets,),
            in_specs=[
                table_spec,
                table_spec,
                pl.BlockSpec((1, depth, 2 * block), lambda f: (f, 0, 0)),
            ],
            out_specs=pl.BlockSpec((1, 2, pix_rows, block), lambda f: (f, 0, 0, 0)),
            out_shape=jax.ShapeDtypeStruct((facets, 2, pix_rows, block), dtype),
            compiler_params=pltpu.CompilerParams(vmem_limit_bytes=56 << 20),
            cost_estimate=pl.CostEstimate(
                flops=8 * facets * pix_rows * depth * block,
                bytes_accessed=8 * facets * pix_rows * depth,
                transcendentals=0,
            ),
            name="column_sums",
        )(col_cos, col_sin, parts)

    swap = [(c, c ^ 1) for c in range(cols)]
    other = lax.ppermute(column_sums(0, BF16), "col", swap)
    summed = column_sums(1, F32) + other.astype(F32)
    return summed * corr_x[None, None, :, None] * corr_y[None, None, None, :]


def solution(mesh):
    in_specs = (
        P(None, ("chan", "col", "row")),
        P(None, None, ("chan", "col", "row")),
        P(("chan", "col", "row"), None),
        P(None, ("chan", "col", "row")),
        P("col"),
        P("row"),
        P(),
    )
    out_specs = P("chan", None, "col", "row")
    return jax.shard_map(body, mesh=mesh, in_specs=in_specs, out_specs=out_specs, check_vma=False)
```

```python
import functools
import math

import jax
import jax.numpy as jnp
from jax import lax
from jax.experimental import pallas as pl
from jax.experimental.pallas import tpu as pltpu
from jax.sharding import PartitionSpec as P

IMAGE = 32768
SUBGRID = 512
FACET = 1536
UNIT = 16
CHUNK = 512
FIELDS = 32
STEP = 32
F32 = jnp.float32
BF16 = jnp.bfloat16
NT = (((1,), (1,)), ((), ()))


def sincos(product):
    quarter = IMAGE // 4
    turn = (product & (IMAGE - 1)) + quarter // 2
    turns = turn // quarter
    x = (turn - turns * quarter - quarter // 2).astype(F32) * (2.0 * math.pi / IMAGE)
    y = x * x
    cosine = 1.0 + y * (-1 / 2 + y * (1 / 24 + y * (-1 / 720 + y * (1 / 40320))))
    sine = x * (1.0 + y * (-1 / 6 + y * (1 / 120 + y * (-1 / 5040 + y * (1 / 362880)))))
    odd = (turns & 1) == 1
    first, second = jnp.where(odd, sine, cosine), jnp.where(odd, cosine, sine)
    flip_cos = ((turns + 1) & 2) == 2
    flip_sin = (turns & 2) == 2
    return jnp.where(flip_cos, -first, first), jnp.where(flip_sin, -second, second)


def coarse_ids(start, count, axis_len):
    steps = lax.broadcasted_iota(jnp.int32, (count // STEP, axis_len), 0)
    return (start + STEP * steps) & (IMAGE - 1)


def fill_table(coarse_cos, coarse_sin, fine, write):
    fine_cos, fine_sin = fine

    def one(step, carry):
        cos_a, sin_a = coarse_cos[pl.ds(step, 1), :], coarse_sin[pl.ds(step, 1), :]
        write(
            pl.ds(pl.multiple_of(step * STEP, STEP), STEP),
            (cos_a * fine_cos - sin_a * fine_sin).astype(BF16),
            (sin_a * fine_cos + cos_a * fine_sin).astype(BF16),
        )
        return carry

    lax.fori_loop(0, coarse_cos.shape[0], one, 0)


def spread_kernel(
    quarter, cols, row_devices, block, facets, win_ref, vis_ref, taps_ref, targets_ref,
    offsets_ref, all_ref, row_table, col_cos, col_sin, *scratch,
):
    row_cos, row_sin, pix_cos, pix_sin = scratch[:4]
    send_row, recv_row, send_chip, recv_chip, send_core, recv_core = scratch[4:]
    own_col, own_row = lax.axis_index("col"), lax.axis_index("row")
    chips = cols // 2
    chip, core = own_col // 2, own_col % 2
    barrier = pltpu.get_barrier_semaphore()
    row_peers = [lax.rem(own_row + k, row_devices) for k in range(1, row_devices)]
    chip_peers = [lax.rem(chip + p, chips) for p in range(1, chips)]
    for peer in row_peers:
        pl.semaphore_signal(
            barrier, inc=1, device_id={"row": peer}, device_id_type=pl.DeviceIdType.MESH
        )
    for peer in chip_peers:
        pl.semaphore_signal(
            barrier, inc=1, device_id={"col": peer * 2 + core}, device_id_type=pl.DeviceIdType.MESH
        )
    pl.semaphore_signal(
        barrier, inc=1, device_id={"col": chip * 2 + 1 - core}, device_id_type=pl.DeviceIdType.MESH
    )

    pack_rows(quarter, vis_ref, taps_ref, targets_ref, offsets_ref, all_ref.at[chip, core, own_row])
    pl.semaphore_wait(barrier, row_devices - 1 + chips - 1 + 1)

    def send(ref, send_sem, recv_sem, device):
        copy = pltpu.make_async_remote_copy(
            src_ref=ref, dst_ref=ref, send_sem=send_sem, recv_sem=recv_sem,
            device_id=device, device_id_type=pl.DeviceIdType.MESH,
        )
        copy.start()
        return copy

    def row_of(k):
        return lax.rem(own_row + row_devices - k, row_devices)

    def to_chips(k):
        ref = all_ref.at[chip, core, row_of(k)]
        return [
            send(
                ref, send_chip.at[k, p - 1], recv_chip.at[k, p - 1],
                {"col": chip_peers[p - 1] * 2 + core},
            )
            for p in range(1, chips)
        ]

    def to_core(k, p):
        ref = all_ref.at[lax.rem(chip + chips - p, chips), core, row_of(k)]
        return send(ref, send_core.at[k, p], recv_core.at[k, p], {"col": chip * 2 + 1 - core})

    by_row = [
        send(
            all_ref.at[chip, core, own_row], send_row.at[k - 1], recv_row.at[k - 1],
            {"row": row_peers[k - 1]},
        )
        for k in range(1, row_devices)
    ]
    by_chip = {0: to_chips(0)}
    by_core = [to_core(0, 0)]

    pix_rows = col_cos.shape[2]
    depth = col_cos.shape[3]
    first_cell = (core * (depth // SUBGRID) - chips) * SUBGRID
    cells = (first_cell + lax.broadcasted_iota(jnp.int32, (1, depth), 1)) & (IMAGE - 1)
    fine_cells = sincos(lax.broadcasted_iota(jnp.int32, (STEP, depth), 0) * cells)
    corner = IMAGE - row_devices // 2 * SUBGRID
    for stage in range(facets + 1):
        if stage == 1:
            for k in range(1, row_devices):
                by_row[k - 1].wait_recv()
                by_chip[k] = to_chips(k)
                by_core.append(to_core(k, 0))
        if stage == 2:
            for k in range(row_devices):
                for p in range(1, chips):
                    by_chip[k][p - 1].wait_recv()
                    by_core.append(to_core(k, p))
        if stage == facets:
            break
        f = stage
        pixels = win_ref[f, 1] + own_row * block + lax.broadcasted_iota(jnp.int32, (1, block), 1)
        fine = sincos(lax.broadcasted_iota(jnp.int32, (STEP, block), 0) * pixels)
        row_cos[...], row_sin[...] = sincos(
            coarse_ids(corner, row_devices * SUBGRID, block) * pixels
        )

        def write_row(place, cosine, sine):
            row_table[place, 2 * f * block : (2 * f + 1) * block] = cosine
            row_table[place, (2 * f + 1) * block : (2 * f + 2) * block] = sine

        fill_table(row_cos, row_sin, fine, write_row)
        for who, holder in enumerate((chip * 2 + 1 - core, own_col)):
            first = win_ref[f, 0] + holder * pix_rows
            pix_cos[...], pix_sin[...] = sincos(coarse_ids(first, pix_rows, depth) * cells)

            def write_col(place, cosine, sine):
                col_cos[f, who, place, :] = cosine
                col_sin[f, who, place, :] = sine

            fill_table(pix_cos, pix_sin, fine_cells, write_col)
    for copy in by_core:
        copy.wait_recv()
    for copy in by_row + [c for k in by_chip for c in by_chip[k]] + by_core:
        copy.wait_send()


def pack_rows(quarter, vis_ref, taps_ref, targets_ref, offsets_ref, out_ref):
    rows = vis_ref.shape[1]
    targets = targets_ref[...]
    named = lax.broadcasted_iota(jnp.int32, (128, rows), 0) == targets
    onehot = jnp.where(named, 1.0, 0.0)
    onehot16 = onehot.astype(BF16)
    counts = lax.dot_general(jnp.ones((16, rows), BF16), onehot16, NT, preferred_element_type=F32)
    units = jnp.floor((counts + (UNIT - 1.0)) * (1.0 / UNIT))
    before = lax.broadcasted_iota(jnp.int32, (128, 128), 0) < lax.broadcasted_iota(
        jnp.int32, (128, 128), 1
    )
    starts = jnp.dot(
        units.astype(BF16), jnp.where(before, 1.0, 0.0).astype(BF16), preferred_element_type=F32
    )
    upto = lax.broadcasted_iota(jnp.int32, (rows, rows), 0) <= lax.broadcasted_iota(
        jnp.int32, (rows, rows), 1
    )
    running = jnp.dot(
        onehot16, jnp.where(upto, 1.0, 0.0).astype(BF16), preferred_element_type=F32
    )
    rank = jnp.sum(running * onehot, axis=0, keepdims=True) - 1.0
    first = jnp.dot(starts.astype(BF16), onehot16, preferred_element_type=F32)[0:1]
    slot = (first * UNIT + rank).astype(jnp.int32)

    lane_pos = lax.broadcasted_iota(jnp.int32, (8, rows), 0)
    placed = []
    for dim in range(2):
        wanted = (lane_pos - offsets_ref[dim : dim + 1, :]) & 7
        value = jnp.zeros((8, rows), F32)
        for tap in range(8):
            row = taps_ref[dim * 8 + tap : dim * 8 + tap + 1, :].astype(F32)
            value = jnp.where(wanted == tap, row, value)
        placed.append(value)
    vis = vis_ref[...].astype(F32)
    offsets = offsets_ref[...]
    upper = (offsets >> 3).astype(F32)
    lower = (offsets & 7).astype(F32)
    extra = jnp.zeros((8, rows), F32)
    for idx, row in enumerate((upper[0:1], lower[0:1], upper[1:2], lower[1:2])):
        extra = jnp.where(lane_pos == idx, row, extra)
    fields = jnp.concatenate(
        [placed[0], placed[1] * vis[0:1], placed[1] * vis[1:2], extra], 0
    ).astype(BF16)
    blank = jnp.zeros_like(fields)
    total = jnp.zeros((quarter, 128), F32)
    slot_ids = lax.broadcasted_iota(jnp.int32, (quarter, rows), 0)
    for part in range(4):
        chosen = jnp.where(slot_ids == slot - part * quarter, 1.0, 0.0).astype(BF16)
        spread = jnp.concatenate([fields if b == part else blank for b in range(4)], 0)
        total += lax.dot_general(chosen, spread, NT, preferred_element_type=F32)
    out_ref[0:quarter, :] = total.astype(BF16)
    which = lax.broadcasted_iota(jnp.int32, (16, 128), 0)
    out_ref[quarter:, :] = jnp.where(
        which == 0, starts, jnp.where(which == 1, units, 0.0)
    ).astype(BF16)


def grid_kernel(
    sources, row_devices, quarter, block, facets,
    starts_ref, units_ref, rows_ref, table_ref, out_ref, packed, grid_sum, grids,
):
    col, row = pl.program_id(0), pl.program_id(1)
    subgrid = col * row_devices + row
    subs = pl.num_programs(0) * row_devices
    per_quarter = quarter // UNIT
    lane_block = lax.broadcasted_iota(jnp.int32, (UNIT, 128), 1) // FIELDS

    def gather(source, pos):
        start = starts_ref[source * subs + subgrid]
        count = units_ref[source * subs + subgrid]

        def batch(step, carry):
            for inner in range(6):
                unit = start + step * 6 + inner
                part = unit // per_quarter
                place = pl.multiple_of((unit - part * per_quarter) * UNIT, UNIT)
                data = rows_ref[source, pl.ds(place, UNIT), :]
                data = jnp.where(lane_block == part, data.astype(F32), 0.0).astype(BF16)
                to = pl.multiple_of((pos + step * 6 + inner) * UNIT, UNIT)
                packed[pl.ds(to, UNIT), :] = data
            return carry

        lax.fori_loop(0, (count + 5) // 6, batch, 0)
        return pos + count

    total = lax.fori_loop(0, sources, gather, 0)
    packed[pl.ds(pl.multiple_of(total * UNIT, UNIT), CHUNK), :] = jnp.zeros((CHUNK, 128), BF16)
    grid_sum[...] = jnp.zeros_like(grid_sum)

    out_row = lax.broadcasted_iota(jnp.int32, (64, 128), 0)
    lane = lax.broadcasted_iota(jnp.int32, (64, 128), 1) % FIELDS
    source_field = jnp.where(out_row < 24, out_row, 24 + (out_row - 24) // 8)
    pick = jnp.where((source_field == lane) & (out_row < 56), 1.0, 0.0).astype(BF16)
    cell = lax.broadcasted_iota(jnp.int32, (8, CHUNK), 0).astype(F32)

    def chunk(step, carry):
        data = packed[pl.ds(pl.multiple_of(step * CHUNK, CHUNK), CHUNK), :]
        field = lax.dot_general(pick, data, NT, preferred_element_type=F32)
        group_u = field[24:32] + jnp.where(cell < field[32:40], 1.0, 0.0)
        group_v = field[40:48] + jnp.where(cell < field[48:56], 1.0, 0.0)
        val_u, val_r, val_i = field[0:8], field[8:16], field[16:24]
        kern_u, kern_r, kern_i = [], [], []
        for g in range(SUBGRID // 8):
            hit_v = group_v == float(g)
            kern_u.append(jnp.where(group_u == float(g), val_u, 0.0))
            kern_r.append(jnp.where(hit_v, val_r, 0.0))
            kern_i.append(jnp.where(hit_v, val_i, 0.0))
        left = jnp.concatenate(kern_u, 0).astype(BF16)
        right = jnp.concatenate(kern_r + kern_i, 0).astype(BF16)
        grid_sum[...] += lax.dot_general(left, right, NT, preferred_element_type=F32)
        return carry

    lax.fori_loop(0, (total * UNIT + CHUNK - 1) // CHUNK, chunk, 0)

    place = pl.ds(pl.multiple_of(row * SUBGRID, SUBGRID), SUBGRID)
    grids[0:SUBGRID, place] = grid_sum[:, :SUBGRID].astype(BF16)
    grids[SUBGRID:, place] = grid_sum[:, SUBGRID:].astype(BF16)

    @pl.when(row == row_devices - 1)
    def _():
        for f in range(facets):
            table = table_ref[:, 2 * f * block : 2 * (f + 1) * block]
            product = jnp.dot(grids[...], table, preferred_element_type=F32)
            real, imag = product[:SUBGRID], product[SUBGRID:]
            out_ref[f, :, :block] = (real[:, :block] - imag[:, block:]).astype(BF16)
            out_ref[f, :, block:] = (real[:, block:] + imag[:, :block]).astype(BF16)


def column_kernel(block, cos_ref, sin_ref, part_ref, out_ref):
    value = part_ref[0]
    first = jnp.dot(cos_ref[0, 0], value, preferred_element_type=F32)
    second = jnp.dot(sin_ref[0, 0], value, preferred_element_type=F32)
    out_ref[0, 0] = (first[:, :block] - second[:, block:]).astype(out_ref.dtype)
    out_ref[0, 1] = (first[:, block:] + second[:, :block]).astype(out_ref.dtype)


def body(visibilities, taps, targets, offsets, corr_x, corr_y, windows):
    cols = lax.axis_size("col")
    row_devices = lax.axis_size("row")
    subgrids = cols * row_devices
    sources = subgrids
    rows = targets.shape[0]
    cap = 3 * rows // subgrids
    half = cols // 2
    own_col = lax.axis_index("col")
    core = lax.rem(own_col, 2)
    facets = windows.shape[0]
    block = FACET // row_devices
    pix_rows = FACET // cols
    quarter = -(-(rows + subgrids * (UNIT - 1)) // (4 * UNIT)) * UNIT

    chips = cols // 2
    depth = half * SUBGRID
    width = facets * 2 * block
    vmem = pl.BlockSpec(memory_space=pltpu.VMEM)
    all_rows, row_table, col_cos, col_sin = pl.pallas_call(
        functools.partial(spread_kernel, quarter, cols, row_devices, block, facets),
        in_specs=[pl.BlockSpec(memory_space=pltpu.SMEM)] + [vmem] * 4,
        out_specs=[vmem] * 4,
        out_shape=[
            jax.ShapeDtypeStruct((chips, 2, row_devices, quarter + 16, 128), BF16),
            jax.ShapeDtypeStruct((row_devices * SUBGRID, width), BF16),
            jax.ShapeDtypeStruct((facets, 2, pix_rows, depth), BF16),
            jax.ShapeDtypeStruct((facets, 2, pix_rows, depth), BF16),
        ],
        scratch_shapes=[pltpu.VMEM((row_devices * SUBGRID // STEP, block), F32)] * 2
        + [pltpu.VMEM((pix_rows // STEP, depth), F32)] * 2
        + [pltpu.SemaphoreType.DMA((max(row_devices - 1, 1),))] * 2
        + [pltpu.SemaphoreType.DMA((row_devices, max(chips - 1, 1)))] * 2
        + [pltpu.SemaphoreType.DMA((row_devices, chips))] * 2,
        compiler_params=pltpu.CompilerParams(
            vmem_limit_bytes=60 << 20, collective_id=0, has_side_effects=True
        ),
        name="spread_rows",
    )(windows, visibilities, taps.reshape(-1, rows), targets.reshape(1, rows), offsets)
    gathered = all_rows.reshape(sources, quarter + 16, 128)

    own_subs = half * row_devices
    meta = gathered[:, quarter : quarter + 2, :].astype(jnp.int32)
    meta = lax.dynamic_slice(meta, (0, 0, core * own_subs), (sources, 2, own_subs))
    starts = meta[:, 0].reshape(-1)
    units = meta[:, 1].reshape(-1)
    room = sources * (-(-cap // UNIT)) * UNIT + CHUNK + 6 * UNIT
    parts = pl.pallas_call(
        functools.partial(grid_kernel, sources, row_devices, quarter, block, facets),
        grid_spec=pltpu.PrefetchScalarGridSpec(
            num_scalar_prefetch=2,
            grid=(half, row_devices),
            in_specs=[
                pl.BlockSpec(
                    (sources, quarter + 16, 128),
                    lambda c, r, *_: (0, 0, 0),
                    pipeline_mode=pl.Buffered(1),
                ),
                pl.BlockSpec(
                    (row_devices * SUBGRID, width),
                    lambda c, r, *_: (0, 0),
                    pipeline_mode=pl.Buffered(1),
                ),
            ],
            out_specs=pl.BlockSpec((facets, SUBGRID, 2 * block), lambda c, r, *_: (0, c, 0)),
            scratch_shapes=[
                pltpu.VMEM((room, 128), BF16),
                pltpu.VMEM((SUBGRID, 2 * SUBGRID), F32),
                pltpu.VMEM((2 * SUBGRID, row_devices * SUBGRID), BF16),
            ],
        ),
        out_shape=jax.ShapeDtypeStruct((facets, half * SUBGRID, 2 * block), BF16),
        compiler_params=pltpu.CompilerParams(vmem_limit_bytes=56 << 20),
        name="grid_rows",
    )(starts, units, gathered, row_table)

    def column_sums(who, dtype):
        table_spec = pl.BlockSpec((1, 1, pix_rows, depth), lambda f: (f, who, 0, 0))
        return pl.pallas_call(
            functools.partial(column_kernel, block),
            grid=(facets,),
            in_specs=[
                table_spec,
                table_spec,
                pl.BlockSpec((1, depth, 2 * block), lambda f: (f, 0, 0)),
            ],
            out_specs=pl.BlockSpec((1, 2, pix_rows, block), lambda f: (f, 0, 0, 0)),
            out_shape=jax.ShapeDtypeStruct((facets, 2, pix_rows, block), dtype),
            compiler_params=pltpu.CompilerParams(vmem_limit_bytes=56 << 20),
            cost_estimate=pl.CostEstimate(
                flops=8 * facets * pix_rows * depth * block,
                bytes_accessed=8 * facets * pix_rows * depth,
                transcendentals=0,
            ),
            name="column_sums",
        )(col_cos, col_sin, parts)

    swap = [(c, c ^ 1) for c in range(cols)]
    other = lax.ppermute(column_sums(0, BF16), "col", swap)
    summed = column_sums(1, BF16).astype(F32) + other.astype(F32)
    return summed * corr_x[None, None, :, None] * corr_y[None, None, None, :]


def solution(mesh):
    in_specs = (
        P(None, ("chan", "col", "row")),
        P(None, None, ("chan", "col", "row")),
        P(("chan", "col", "row"), None),
        P(None, ("chan", "col", "row")),
        P("col"),
        P("row"),
        P(),
    )
    out_specs = P("chan", None, "col", "row")
    return jax.shard_map(body, mesh=mesh, in_specs=in_specs, out_specs=out_specs, check_vma=False)
```
